512 devices in a mesh: axial: 16 (over y_lo, x, core), circ: 32 (over z, y_hi).
Axes of the slice: x: 4, y: 4 (y_hi: 2, y_lo: 2; y = y_hi * 2 + y_lo), z: 16, core: 2. Of those that a mesh axis runs over, the one named last changes fastest.
Arguments:
- lam_h: bfloat16 [32, 64, 128, 512], P('axial', 'circ'), may hold values from -6 to 6
- lam_v: bfloat16 [32, 64, 128, 512], P('axial', 'circ'), may hold values from -6 to 6
- panel: bfloat16 [32, 64, 512, 512], P('axial', 'circ')
- corner_panel: bfloat16 [32, 64, 512, 128], P('axial', 'circ'), may hold values from -0.25 to 0.25
- coarse_diag: float32 [32, 128, 128], P('axial'), may hold values from -0.0625 to 0.0625
- coarse_link: float32 [32, 128, 128], P('axial')
- edge_slot: int32 [32, 64, 4], P('axial', 'circ'), may hold values from 0 to 3, as said below
Outputs:
- jump_h: bfloat16 [32, 64, 128, 512], P('axial', 'circ')
- jump_v: bfloat16 [32, 64, 128, 512], P('axial', 'circ')
The draws below stay inside these ranges and needn't reach their ends.
Inputs may be any that keep to these rules, and one draw needn't show every extreme that they name: For each subdomain (a, c) the four entries edge_slot[a, c, 0], ..., edge_slot[a, c, 3] are 0, 1, 2, 3 in some order, drawn independently for each subdomain; within a subdomain row each value occurs 64 times.
All inputs are finite; a program needn't handle non-finite values.
Results may differ from the reference program's by a relative error of at most 0.0061.
Values may be sent and summed in bfloat16 or wider, within the bound.
No kernel may reach another device: no remote copies, remote signals or barrier semaphores. Data moves between devices by JAX's collectives and lax.ppermute only.
A program may use at most 64 MiB of HBM per device.

```python
import math
import jax
import jax.numpy as jnp
from jax import lax

E = 128
P_SIZE = 512
NCOR = 128
R = 512
NA = 32
NC = 64


def draw_panel(key, part):
    noise_key = jax.random.fold_in(key, 11)
    noise = jax.random.normal(noise_key, (NA, NC, P_SIZE, P_SIZE), jnp.float32)
    identity = (lax.broadcasted_iota(jnp.int32, (P_SIZE, P_SIZE), 0) == lax.broadcasted_iota(jnp.int32, (P_SIZE, P_SIZE), 1)).astype(jnp.float32)
    return (identity + 0.6 * noise / math.sqrt(P_SIZE)).astype(jnp.bfloat16)


def draw_coarse_link(key, part):
    noise_key = jax.random.fold_in(key, 23)
    noise = jax.random.normal(noise_key, (NA, NCOR, NCOR), jnp.float32)
    identity = (lax.broadcasted_iota(jnp.int32, (NCOR, NCOR), 0) == lax.broadcasted_iota(jnp.int32, (NCOR, NCOR), 1)).astype(jnp.float32)
    return 0.95 * identity + 0.3 * noise / math.sqrt(NCOR)


def draw_edge_slot(key, part):
    slot_key = jax.random.fold_in(key, 37)
    keys = jax.random.split(slot_key, NA * NC)
    orders = jax.vmap(lambda single: jax.random.permutation(single, 4))(keys)
    return orders.astype(jnp.int32).reshape(NA, NC, 4)


def levels(rng, extent, shards, smallest, top_value):
    loudness = 1.0
    for dim, parts in shards:
        draws = jax.random.uniform(jax.random.fold_in(jax.random.fold_in(rng, 6), dim), (parts,), jnp.float32, smallest / len(shards), top_value / len(shards))
        loudness = loudness * jnp.repeat(jnp.exp(draws), extent[dim] // parts).reshape((-1,) + (1,) * (len(extent) - 1 - dim))
    return loudness


def gaussian(stream_key, extent, spread, reach, cuts=(), kind=jnp.bfloat16):
    array = jax.random.normal(stream_key, extent, jnp.float32) * spread
    if len(cuts) > 0:
        array = levels(stream_key, extent, cuts, -0.22, 0.18) * array
    return jnp.clip(array, min=-reach, max=reach).astype(kind)


def setup_inputs(seed: int = 0) -> dict:
    arg_keys = jax.random.split(jax.random.key(seed), 8)
    lam_h = gaussian(arg_keys[0], (NA, NC, E, R), 1.0, 6.0, ((0, 16), (1, 32)))
    lam_v = gaussian(arg_keys[1], (NA, NC, E, R), 1.0, 6.0, ((0, 16), (1, 32)))
    panel = draw_panel(jax.random.fold_in(arg_keys[7], 71), 0)
    corner_panel = gaussian(arg_keys[3], (NA, NC, P_SIZE, NCOR), P_SIZE ** -0.5, 0.25, ((0, 16), (1, 32)))
    coarse_diag = gaussian(arg_keys[4], (NA, NCOR, NCOR), (NCOR * NC) ** -0.5, 0.0625, ((0, 16),), jnp.float32)
    coarse_link = draw_coarse_link(jax.random.fold_in(arg_keys[7], 71), 0)
    edge_slot = draw_edge_slot(jax.random.fold_in(arg_keys[7], 71), 0)
    return dict(lam_h=lam_h, lam_v=lam_v, panel=panel, corner_panel=corner_panel, coarse_diag=coarse_diag, coarse_link=coarse_link, edge_slot=edge_slot)


def reference(lam_h, lam_v, panel, corner_panel, coarse_diag, coarse_link, edge_slot):
    highest = lax.Precision.HIGHEST
    lower_h = jnp.roll(lam_h, 1, axis=1)
    lower_v = jnp.concatenate([jnp.zeros_like(lam_v[:1]), lam_v[:-1]], axis=0)
    edges = jnp.stack([lam_h, -lower_h, lam_v, -lower_v], axis=2)
    slots = (edge_slot[..., None] == jnp.arange(4, dtype=jnp.int32)).astype(jnp.float32)
    placed = jnp.einsum('abkj,abker->abjer', slots, edges.astype(jnp.float32), precision=highest)
    placed = placed.astype(jnp.bfloat16).reshape(NA, NC, P_SIZE, R)

    def row_solve(items):
        pan, plc, cor = items
        flexed_row = jnp.einsum('cpq,cpr->cqr', pan.astype(jnp.float32), plc.astype(jnp.float32), precision=highest)
        rounded = lax.optimization_barrier(flexed_row.astype(jnp.bfloat16))
        partial_row = jnp.einsum('cpk,cpr->kr', cor.astype(jnp.float32), rounded.astype(jnp.float32), precision=highest)
        return flexed_row, partial_row

    flexed, totals = lax.map(row_solve, (panel, placed, corner_panel))

    def sweep_step(carry, items):
        diag_block, link_block, total_row = items
        value = jnp.dot(diag_block, total_row, precision=highest) + jnp.dot(link_block, carry, precision=highest)
        return value, value

    _, coarse = lax.scan(sweep_step, jnp.zeros((NCOR, R), jnp.float32), (coarse_diag, coarse_link, totals), reverse=True)
    correction = coarse.astype(jnp.bfloat16)

    def row_pick(items):
        flexed_row, cor, corr_row, slot_row = items
        update = flexed_row - jnp.einsum('cpk,kr->cpr', cor.astype(jnp.float32), corr_row.astype(jnp.float32), precision=highest)
        update = lax.optimization_barrier(update.astype(jnp.bfloat16)).reshape(NC, 4, E, R)
        choose = (slot_row[..., None] == jnp.arange(4, dtype=jnp.int32)).astype(jnp.float32)
        return jnp.einsum('ckj,cjer->cker', choose, update.astype(jnp.float32), precision=highest).astype(jnp.bfloat16)

    picked = lax.map(row_pick, (flexed, corner_panel, correction, edge_slot))
    next_left = jnp.roll(picked[:, :, 1], -1, axis=1)
    next_down = jnp.concatenate([picked[1:, :, 3], jnp.zeros_like(picked[:1, :, 3])], axis=0)
    jump_h = (picked[:, :, 0].astype(jnp.float32) - next_left.astype(jnp.float32)).astype(jnp.bfloat16)
    jump_v = (picked[:, :, 2].astype(jnp.float32) - next_down.astype(jnp.float32)).astype(jnp.bfloat16)
    return (jump_h, jump_v)
```

```python
import jax
import jax.numpy as jnp
from jax import lax
from jax.experimental import pallas as pl
from jax.experimental.pallas import tpu as pltpu
from jax.sharding import Mesh, PartitionSpec as P

E = 128
P_SIZE = 512
NCOR = 128
R = 512
SPLIT = (2, 4, 2, 16, 2)
AXIAL = ("ylo", "x", "core")
CIRC = ("z", "yhi")
CHIPS = ("ylo", "x")
PLANE = ("ylo", "x", "core", "yhi")
F32 = jnp.float32
BF16 = jnp.bfloat16
HIGHEST = lax.Precision.HIGHEST


def dot(a, b, ca=1, cb=0, precision=None):
    return lax.dot_general(
        a, b, (((ca,), (cb,)), ((), ())), preferred_element_type=F32, precision=precision
    )


def split2(value):
    high = value.astype(BF16)
    return high, (value - high.astype(F32)).astype(BF16)


def dot_nt3(a, b_high, b_low):
    a_high, a_low = split2(a)
    return dot(a_high, b_high, 1, 1) + dot(a_high, b_low, 1, 1) + dot(a_low, b_high, 1, 1)


def rows(slot, a, c, k):
    return pl.ds(pl.multiple_of(slot[a, c, k] * E, E), E)


def prep_kernel(slot, panel, corner, lam_h, lam_v, part, w1, w3):
    w = {}
    for a in range(2):
        for c in range(2):
            for k in range(4):
                w[a, c, k] = dot(panel[a, c, rows(slot, a, c, k), :], corner[a, c])
    for i in range(2):
        w1[i] = w[i, 0, 1].astype(BF16)
        w3[i] = w[0, i, 3].astype(BF16)
    wh = [
        jnp.concatenate([w[a, 0, 0] - w[a, 1, 1], w[a, 1, 0]], axis=0).astype(BF16)
        for a in range(2)
    ]
    wv = [jnp.concatenate([w[a, 0, 2], w[a, 1, 2]], axis=0).astype(BF16) for a in range(2)]
    wl = jnp.concatenate([w[1, 0, 3], w[1, 1, 3]], axis=0).astype(BF16)
    part[:, :NCOR] = dot(lam_h[0], wh[0], 0, 0) + dot(lam_v[0], wv[0], 0, 0)
    part[:, NCOR:] = (
        dot(lam_h[1], wh[1], 0, 0) + dot(lam_v[1], wv[1], 0, 0) - dot(lam_v[0], wl, 0, 0)
    )


def halo_kernel(part, w1, w3, left, below, out):
    out[:, :NCOR] = (
        part[:, :NCOR]
        - dot(left[0], w1[0], 0, 0)
        - dot(below[0], w3[0], 0, 0)
        - dot(below[1], w3[1], 0, 0)
    ).astype(BF16)
    out[:, NCOR:] = (part[:, NCOR:] - dot(left[1], w1[1], 0, 0)).astype(BF16)


def flex_kernel(
    slot, panel, corner, lam_h, lam_v, left, below, base_h, base_v, send_h, send_v, placed, flexed
):
    for a in range(2):
        for c in range(2):
            edges = (
                lam_h[a, c],
                -(lam_h[a, 0] if c else left[a]),
                lam_v[a, c],
                -(lam_v[0, c] if a else below[c]),
            )
            for k in range(4):
                placed[rows(slot, a, c, k), :] = edges[k]
            flexed[...] = dot(panel[a, c], placed[...], 0, 0)
            base_h[a, c] = flexed[rows(slot, a, c, 0), :]
            base_v[a, c] = flexed[rows(slot, a, c, 2), :]
            left_block = flexed[rows(slot, a, c, 1), :]
            down_block = flexed[rows(slot, a, c, 3), :]
            if c:
                base_h[a, 0] = base_h[a, 0] - left_block
            else:
                send_h[a, :, :R] = left_block.astype(BF16)
                send_h[a, :, R:] = corner[a, c, rows(slot, a, c, 1), :]
            if a:
                base_v[0, c] = base_v[0, c] - down_block
            else:
                send_v[c, :, :R] = down_block.astype(BF16)
                send_v[c, :, R:] = corner[a, c, rows(slot, a, c, 3), :]


def pair_kernel(link, pair):
    pair[...] = dot(link[0], link[1], precision=HIGHEST)


def chip_kernel(is_core_1, diag, link, pair, other, chip, terms):
    core_1 = is_core_1[0] == 1
    first = jnp.where(core_1, other[...], pair[...])
    second = jnp.where(core_1, pair[...], other[...])
    value = dot(first, second, precision=HIGHEST)
    for m in range(chip.shape[0]):
        chip[m] = value
    lower = dot(link[0], diag[1], precision=HIGHEST)
    seen_0 = jnp.where(core_1, dot(other[...], diag[0], precision=HIGHEST), diag[0])
    seen_1 = jnp.where(core_1, dot(other[...], lower, precision=HIGHEST), lower)
    table = (
        (seen_0, seen_1),
        (diag[0], lower),
        (jnp.zeros_like(lower), diag[1]),
    )
    for i in range(3):
        for j in range(2):
            high, low = split2(table[i][j])
            place = (slice(i * NCOR, (i + 1) * NCOR), slice(j * NCOR, (j + 1) * NCOR))
            terms[(0, *place)] = high
            terms[(1, *place)] = low


def chain_kernel(where, other, pair, link, chips, chain, own):
    count = chips.shape[0]
    me, core_1 = where[0], where[1] == 1
    eye = (
        lax.broadcasted_iota(jnp.int32, (NCOR, NCOR), 0)
        == lax.broadcasted_iota(jnp.int32, (NCOR, NCOR), 1)
    ).astype(F32)
    value = jnp.where(core_1, eye, other[...])
    for j in range(1, count):
        if j > 1:
            value = dot(value, chips[jnp.minimum(me + j - 1, count - 1)], precision=HIGHEST)
        high, low = split2(jnp.where(me + j < count, value, 0.0))
        chain[0, :, (j - 1) * NCOR : j * NCOR] = high
        chain[1, :, (j - 1) * NCOR : j * NCOR] = low
    for i, matrix in enumerate((pair[...], link[1])):
        high, low = split2(matrix)
        own[0, i * NCOR : (i + 1) * NCOR, :] = high
        own[1, i * NCOR : (i + 1) * NCOR, :] = low


def sum_kernel(where, received, terms, out):
    total = received[0].astype(F32)
    for i in range(1, received.shape[0]):
        total = total + received[i].astype(F32)
    value = dot_nt3(total, terms[0], terms[1])
    seen = value[:, :NCOR].astype(BF16)
    mine = value[:, NCOR : 2 * NCOR].astype(BF16)
    upper = value[:, 2 * NCOR :].astype(BF16)
    for p in range(out.shape[0]):
        out[p, :, :NCOR] = jnp.where(where[0] == p // 4, mine, seen)
        out[p, :, NCOR:] = upper


def carry_kernel(where, received, chain, own, out):
    count = received.shape[0] // 4
    me, core_1 = where[0], where[1] == 1

    def summed(first, number, columns):
        total = received[first, :, columns].astype(F32)
        for i in range(1, number):
            total = total + received[first + i, :, columns].astype(F32)
        return total

    left, right = slice(0, NCOR), slice(NCOR, 2 * NCOR)
    above = jnp.concatenate(
        [summed(4 * jnp.minimum(me + j, count - 1), 4, left) for j in range(1, count)], axis=1
    )
    carry = dot_nt3(above, chain[0], chain[1])
    upper_core = summed(4 * me + 2, 2, left)
    carry = carry + jnp.where(core_1, 0.0, upper_core)
    mine = 4 * me + 2 * where[1]
    both = dot_nt3(carry, own[0], own[1])
    row_0 = (summed(mine, 2, left) + both[:, :NCOR]).astype(BF16)
    row_1 = (summed(mine, 2, right) + both[:, NCOR:]).astype(BF16)
    row_2 = carry.astype(BF16)
    for p in range(out.shape[0]):
        out[p, :, :NCOR] = row_0
        out[p, :, NCOR : 2 * NCOR] = row_1
        out[p, :, 2 * NCOR :] = row_2


def jump_kernel(slot, corner, base_h, base_v, from_right, from_above, corr, jump_h, jump_v):
    def block(a, c, k):
        return corner[a, c, rows(slot, a, c, k), :]

    for a in range(2):
        this = corr[:, a * NCOR : (a + 1) * NCOR]
        twice = jnp.concatenate([this, this], axis=1)
        pair = corr[:, a * NCOR : (a + 2) * NCOR]
        for c in range(2):
            left = from_right[a, :, R:] if c else block(a, 1, 1)
            right = jnp.concatenate([block(a, c, 0), -left], axis=1)
            value = base_h[a, c] - dot(right, twice, 1, 1)
            if c:
                value = value - from_right[a, :, :R].astype(F32)
            jump_h[a, c] = value.astype(BF16)
            down = from_above[c, :, R:] if a else block(1, c, 3)
            right = jnp.concatenate([block(a, c, 2), -down], axis=1)
            value = base_v[a, c] - dot(right, pair, 1, 1)
            if a:
                value = value - from_above[c, :, :R].astype(F32)
            jump_v[a, c] = value.astype(BF16)


def call(kernel, outs, ins, smem=(), flops=0, scratch=()):
    shapes = [jax.ShapeDtypeStruct(shape, dtype) for shape, dtype in outs]
    size = sum(x.size * x.dtype.itemsize for x in list(ins) + shapes)
    result = pl.pallas_call(
        kernel,
        out_shape=shapes,
        in_specs=[
            pl.BlockSpec(memory_space=pltpu.SMEM if i in smem else pltpu.VMEM)
            for i in range(len(ins))
        ],
        out_specs=[pl.BlockSpec(memory_space=pltpu.VMEM)] * len(outs),
        scratch_shapes=list(scratch),
        compiler_params=pltpu.CompilerParams(vmem_limit_bytes=14 * 1024 * 1024),
        cost_estimate=pl.CostEstimate(flops=flops, bytes_accessed=size, transcendentals=0),
    )(*ins)
    return result[0] if len(outs) == 1 else result


def around(value, axes, by):
    count = lax.axis_size(axes)
    return lax.ppermute(value, axes, [(i, (i + by) % count) for i in range(count)])


def along(value, axes, by):
    count = lax.axis_size(axes)
    pairs = [(i, i + by) for i in range(count) if 0 <= i + by < count]
    return lax.ppermute(value, axes, pairs)


def on_device(lam_h, lam_v, panel, corner, diag, link, slot):
    nz, chips, plane = lax.axis_size("z"), lax.axis_size(CHIPS), lax.axis_size(PLANE)
    cols = R // nz
    where = jnp.stack([lax.axis_index(CHIPS), lax.axis_index("core")]).astype(jnp.int32)
    flat_h, flat_v = lam_h.reshape(2, 2 * E, R), lam_v.reshape(2, 2 * E, R)

    left = around(lam_h[:, 1], CIRC, 1)
    below = along(lam_v[1], AXIAL, 1)

    pair = call(pair_kernel, [((NCOR, NCOR), F32)], [link], flops=6 * 2 * NCOR**3)
    other = around(pair, "core", 1)

    part, w1, w3 = call(
        prep_kernel,
        [((R, 2 * NCOR), F32), ((2, E, NCOR), BF16), ((2, E, NCOR), BF16)],
        [slot, panel, corner, flat_h, flat_v],
        smem=(0,),
        flops=2 * (4 * P_SIZE * P_SIZE * NCOR + 10 * E * R * NCOR),
    )
    partial = call(
        halo_kernel,
        [((R, 2 * NCOR), BF16)],
        [part, w1, w3, left, below],
        flops=2 * 4 * E * R * NCOR,
    )
    scattered = lax.all_to_all(partial.reshape(nz, cols, 2 * NCOR), "z", 0, 0)

    chip, terms = call(
        chip_kernel,
        [((chips, NCOR, NCOR), F32), ((2, 3 * NCOR, 2 * NCOR), BF16)],
        [where[1:], diag, link, pair, other],
        smem=(0,),
        flops=6 * 4 * 2 * NCOR**3,
    )
    every_chip = lax.all_to_all(chip, CHIPS, 0, 0)
    chain, own = call(
        chain_kernel,
        [((2, NCOR, (chips - 1) * NCOR), BF16), ((2, 2 * NCOR, NCOR), BF16)],
        [where, other, pair, link, every_chip],
        smem=(0,),
        flops=6 * chips * 2 * NCOR**3,
    )

    base_h, base_v, send_h, send_v = call(
        flex_kernel,
        [((2, 2, E, R), F32)] * 2 + [((2, E, R + NCOR), BF16)] * 2,
        [slot, panel, corner, lam_h, lam_v, left, below],
        smem=(0,),
        flops=4 * 2 * P_SIZE * P_SIZE * R,
        scratch=[pltpu.VMEM((P_SIZE, R), BF16), pltpu.VMEM((P_SIZE, R), F32)],
    )
    from_right = around(send_h, CIRC, -1)
    from_above = along(send_v, AXIAL, -1)

    vectors = call(
        sum_kernel,
        [((plane, cols, 2 * NCOR), BF16)],
        [where, scattered, terms],
        smem=(0,),
        flops=3 * 2 * cols * 6 * NCOR**2,
    )
    gathered = lax.all_to_all(vectors, PLANE, 0, 0)
    mine = call(
        carry_kernel,
        [((nz, cols, 3 * NCOR), BF16)],
        [where, gathered, chain, own],
        smem=(0,),
        flops=3 * 2 * cols * (chips + 2) * NCOR**2,
    )
    corr = lax.all_to_all(mine, "z", 0, 0).reshape(R, 3 * NCOR)
    jump_h, jump_v = call(
        jump_kernel,
        [((2, 2, E, R), BF16)] * 2,
        [slot, corner, base_h, base_v, from_right, from_above, corr],
        smem=(0,),
        flops=2 * 8 * E * R * 2 * NCOR,
    )
    return jump_h, jump_v


def solution(mesh):
    fine = Mesh(mesh.devices.reshape(SPLIT), AXIAL + CIRC)
    return jax.shard_map(
        on_device,
        mesh=fine,
        in_specs=(P(AXIAL, CIRC),) * 4 + (P(AXIAL),) * 2 + (P(AXIAL, CIRC),),
        out_specs=(P(AXIAL, CIRC),) * 2,
        check_vma=False,
    )
```
